512 devices in a mesh: row: 32 (over z_hi, x, y), col: 16 (over z_lo, core).
Axes of the slice: x: 4, y: 4, z: 16 (z_hi: 2, z_lo: 8; z = z_hi * 8 + z_lo), core: 2. Of those that a mesh axis runs over, the one named last changes fastest.
Arguments:
- a_blocks: float32 [128, 32, 128, 128], P('row', 'col'), may hold values from -0.09375 to 0.09375
- b_blocks: float32 [32, 64, 128, 128], P('row', 'col'), may hold values from -6 to 6
- a_occupied: int32 [128, 32], P('row', 'col'), may hold values from 0 to 1, as said below
- b_occupied: int32 [32, 64], P('row', 'col'), may hold values 0 or 1
- c_filter: int32 [128, 64], P('row', 'col'), may hold values 0 or 1
- row_sizes: int32 [128], P('row'), may hold values from 32 to 128, as said below
- k_sizes: int32 [32], replicated, may hold values from 32 to 128, as said below
- col_sizes: int32 [64], P('col'), may hold values from 32 to 128, as said below
Outputs:
- c_product: float32 [128, 64, 128, 128], P('row', 'col')
The draws below stay inside these ranges and needn't reach their ends.
Inputs may be any that keep to these rules, and one draw needn't show every extreme that they name: `a_occupied`: at most 6 of the 4 x 2 blocks that one device holds are occupied, and some device holds exactly 6. `row_sizes`: some block row uses all 128 rows. `k_sizes`: some inner block index uses all 128 rows. `col_sizes`: some block column uses all 128 columns.
All inputs are finite; a program needn't handle non-finite values. No bound on the sum of `b_occupied` or of `c_filter` on one device may be relied on, other than what follows from the above.
Results may differ from the reference program's by a relative error of at most 0.00007.
Values sent between devices are 32-bit elements; how exact they have to be, the bound alone decides.
No kernel may reach another device: no remote copies, remote signals or barrier semaphores. Data moves between devices by JAX's collectives and lax.ppermute only.
A program may use at most 64 MiB of HBM per device.

```python
import jax
import jax.numpy as jnp
from jax import lax

BS = 128
IB = 4
NI = 128
NJ = 64
NK = 32
KB = 2
CAP = 6


def sized_entries(key, count):
    values = jax.random.randint(key, (count,), BS // 4, BS + 1)
    where_full = jax.random.randint(jax.random.fold_in(key, 7), (), 0, count)
    return values.at[where_full].set(BS).astype(jnp.int32)


def draw_row_sizes(key, part):
    key = jax.random.fold_in(key, 1)
    return sized_entries(key, NI)


def draw_k_sizes(key, part):
    key = jax.random.fold_in(key, 2)
    return sized_entries(key, NK)


def draw_col_sizes(key, part):
    key = jax.random.fold_in(key, 3)
    return sized_entries(key, NJ)


def draw_a_occupied(key, part):
    key = jax.random.fold_in(key, 4)
    groups_row = NI // IB
    groups_col = NK // KB
    groups = groups_row * groups_col
    per_group = IB * KB
    count_key, full_key, rank_key = jax.random.split(key, 3)
    counts = jax.random.randint(count_key, (groups,), 1, CAP + 1)
    where_full = jax.random.randint(full_key, (), 0, groups)
    counts = counts.at[where_full].set(CAP)
    group_keys = jax.random.split(rank_key, groups)

    def ranking(group_key):
        return jax.random.permutation(group_key, per_group)
    ranks = jax.vmap(ranking)(group_keys)
    occupied = (ranks < counts[:, None]).astype(jnp.int32)
    occupied = occupied.reshape(groups_row, groups_col, IB, KB).transpose(0, 2, 1, 3)
    return occupied.reshape(NI, NK)


def set_ends(values, key, smallest, top_value):
    longest = values.shape.index(max(values.shape))
    spots = []
    for shift in (0, 1):
        where = [jax.random.randint(jax.random.fold_in(key, axis), (), 0, length) for axis, length in enumerate(values.shape)]
        where[longest] = (where[longest] + shift) % values.shape[longest]
        spots.append(tuple(where))
    return values.at[spots[0]].set(smallest).at[spots[1]].set(top_value)


def steps_of(key, dims, cuts, low, high):
    factor_of, own = 1.0, jax.random.fold_in(key, 6)
    for position, blocks in cuts:
        draws = jnp.exp(jax.random.uniform(jax.random.fold_in(own, position), (blocks,), jnp.float32, low / len(cuts), high / len(cuts)))
        factor_of = factor_of * jnp.repeat(draws, dims[position] // blocks).reshape([-1 if axis == position else 1 for axis in range(len(dims))])
    return factor_of


def bell_draw(stream_key, shape, deviation, bound, shards=(), kind=jnp.bfloat16):
    array = jax.random.normal(stream_key, shape, jnp.float32) * deviation
    if len(shards) > 0:
        array = steps_of(stream_key, shape, shards, -0.22, 0.18) * array
    return jnp.clip(array, min=-bound, max=bound).astype(kind)


def setup_inputs(seed: int = 0) -> dict:
    splits = jax.random.split(jax.random.key(seed), 9)
    return {
        "a_blocks": bell_draw(splits[0], (NI, NK, BS, BS), (NK * BS) ** -0.5, 0.09375, ((0, 32), (1, 16)), jnp.float32),
        "b_blocks": bell_draw(splits[1], (NK, NJ, BS, BS), 1.0, 6.0, ((0, 32), (1, 16)), jnp.float32),
        "a_occupied": draw_a_occupied(jax.random.fold_in(splits[8], 71), 0),
        "b_occupied": set_ends((jax.random.randint(splits[3], (NK, NJ), 0, 4) < 3).astype(jnp.int32), jax.random.fold_in(splits[3], 1), 0, 1),
        "c_filter": set_ends((jax.random.randint(splits[4], (NI, NJ), 0, 4) < 3).astype(jnp.int32), jax.random.fold_in(splits[4], 1), 0, 1),
        "row_sizes": draw_row_sizes(jax.random.fold_in(splits[8], 71), 0),
        "k_sizes": draw_k_sizes(jax.random.fold_in(splits[8], 71), 0),
        "col_sizes": draw_col_sizes(jax.random.fold_in(splits[8], 71), 0),
    }


def masked_blocks(blocks, occupied, row_used, col_used):
    size = blocks.shape[-1]
    line = jnp.arange(size, dtype=jnp.int32)
    rows_fine = line[None, None, :, None] < row_used[:, None, None, None]
    cols_fine = line[None, None, None, :] < col_used[None, :, None, None]
    keep = (occupied[:, :, None, None] > 0) & rows_fine & cols_fine
    return jnp.where(keep, blocks, jnp.zeros_like(blocks))


def reference(a_blocks, b_blocks, a_occupied, b_occupied, c_filter, row_sizes, k_sizes, col_sizes):
    left = masked_blocks(a_blocks, a_occupied, row_sizes, k_sizes)
    right = masked_blocks(b_blocks, b_occupied, k_sizes, col_sizes)

    def one_row(left_row):
        return jnp.einsum("kab,kjbc->jac", left_row, right, precision=lax.Precision.HIGHEST)

    product = lax.map(one_row, left)
    return jnp.where(c_filter[:, :, None, None] > 0, product, jnp.zeros_like(product))
```

```python
import functools

import jax
import jax.numpy as jnp
from jax import lax
from jax.experimental import pallas as pl
from jax.experimental.pallas import tpu as pltpu
from jax.sharding import PartitionSpec as P

BS = 128
CAP = 6
SLOT_ROWS = CAP * BS
PAY_ROWS = SLOT_ROWS + 8
HALF_ROWS = 8 * BS
AXES = ("row", "col")
NX, NY, NZH, NZL, NC = 4, 4, 2, 8, 2


def device_pairs(move):
    pairs = []
    for zh in range(NZH):
        for x in range(NX):
            for y in range(NY):
                for zl in range(NZL):
                    for core in range(NC):
                        to = move(zh, x, y, zl, core)
                        pairs.append((linear(zh, x, y, zl, core), linear(*to)))
    return pairs


def linear(zh, x, y, zl, core):
    return (((zh * NX + x) * NY + y) * NZL + zl) * NC + core


def along_x(n):
    return device_pairs(lambda zh, x, y, zl, core: (zh, (x + n) % NX, y, zl, core))


def along_y(n):
    return device_pairs(lambda zh, x, y, zl, core: (zh, x, (y + n) % NY, zl, core))


def other_half():
    return device_pairs(lambda zh, x, y, zl, core: (1 - zh, x, y, zl, core))


def other_core():
    return device_pairs(lambda zh, x, y, zl, core: (zh, x, y, zl, 1 - core))


def send(value, pairs):
    return lax.ppermute(value, AXES, pairs)


def near(block, along):
    return send(block, along(1)), send(block, along(-1)), send(block, along(2))


def gather_far(group, along):
    half = group.shape[0] // 2
    below = send(group, along(1))
    above = send(group, along(-1))
    return below, above, send(below[:half], along(1)), send(above[half:], along(-1))


def pack_left(blocks, occupied, row_sizes, k_sizes, out):
    first_k = lax.axis_index("col") * 2
    line = lax.broadcasted_iota(jnp.int32, (BS, BS), 0)
    lane = lax.broadcasted_iota(jnp.int32, (BS, BS), 1)
    slot = jnp.int32(0)
    for i in range(4):
        for k in range(2):
            here = (occupied[i, k] > 0) & (slot < CAP)
            place = slot

            @pl.when(here)
            def _():
                keep = (line < row_sizes[i]) & (lane < k_sizes[first_k + k])
                start = pl.multiple_of(place * BS, BS)
                out[pl.ds(start, BS), :] = jnp.where(keep, blocks[i, k], 0.0)

            where = jnp.where(here, place, -1).astype(jnp.float32)
            out[SLOT_ROWS + 2 * i + k, :] = jnp.full((BS,), where, jnp.float32)
            slot = slot + here.astype(jnp.int32)


def mask_right(blocks, occupied, k_sizes, col_sizes, out):
    used = k_sizes[lax.axis_index("row")]
    line = lax.broadcasted_iota(jnp.int32, (BS, BS), 0)
    lane = lax.broadcasted_iota(jnp.int32, (BS, BS), 1)
    for j in range(4):
        columns = jnp.where(occupied[0, j] > 0, col_sizes[j], 0)
        out[j * BS:(j + 1) * BS, :] = jnp.where((line < used) & (lane < columns), blocks[0, j], 0.0)


def split(value):
    high = value.astype(jnp.bfloat16)
    return high, (value - high.astype(jnp.float32)).astype(jnp.bfloat16)


NEAR = (0, -1, 1, 2)


def prepare_right(pieces, own_family, high_out, low_out):
    row, core = lax.axis_index("row"), lax.axis_index("col") % 2
    x, y = (row // 4) % 4, row % 4
    for step in range(4):
        for t in range(4):
            ref, at = (pieces[step], t) if step < 3 else (pieces[3 + t // 2], t % 2)
            across, along = (NEAR[t], NEAR[step]) if own_family else (NEAR[step], NEAR[t])
            from_x, from_y = (x + across + 4) % 4, (y + along + 4) % 4
            foreign = (from_y // 2 != core).astype(jnp.int32)
            start = pl.multiple_of(foreign * HALF_ROWS + from_x * 2 * BS + from_y % 2 * BS, BS)
            for j in range(4):
                high, low = split(ref[(4 * at + j) * BS:(4 * at + j + 1) * BS, :])
                high_out[pl.ds(start, BS), j * BS:(j + 1) * BS] = high
                low_out[pl.ds(start, BS), j * BS:(j + 1) * BS] = low


def multiply(panel, rights, ready, places, copied, left_high, left_low):
    zh = lax.axis_index("row") // 16
    dot = functools.partial(jnp.dot, preferred_element_type=jnp.float32)
    total = None
    for family in range(2):
        half = zh if family == 0 else 1 - zh
        for x in range(4):
            zl = half * 4 + x
            wide = 2 * BS * (4 * family + x)
            for i in range(4):
                for k in range(2):
                    slot = places[zl, 2 * i + k, 0].astype(jnp.int32)
                    start = pl.multiple_of(zl * PAY_ROWS + jnp.maximum(slot, 0) * BS, 8)
                    block_high, block_low = split(jnp.where(slot >= 0, panel[pl.ds(start, BS), :], 0.0))
                    left_high[i * BS:(i + 1) * BS, wide + k * BS:wide + (k + 1) * BS] = block_high
                    left_low[i * BS:(i + 1) * BS, wide + k * BS:wide + (k + 1) * BS] = block_low
    for family in range(2):
        ready(family)
        high, low = rights[2 * family], rights[2 * family + 1]
        for x in range(4):
            wide = 2 * BS * (4 * family + x)
            right_high, right_low = high[2 * BS * x:2 * BS * (x + 1), :], low[2 * BS * x:2 * BS * (x + 1), :]
            here_high = left_high[:, wide:wide + 2 * BS]
            part = dot(here_high, right_high) + dot(here_high, right_low)
            part = part + dot(left_low[:, wide:wide + 2 * BS], right_high)
            total = part if total is None else total + part
    return total


def copy_places(panel, places, copied):
    copies = [
        pltpu.make_async_copy(panel.at[pl.ds(zl * PAY_ROWS + SLOT_ROWS, 8)], places.at[zl], copied.at[zl])
        for zl in range(NZL)
    ]
    for copy in copies:
        copy.start()
    for copy in copies:
        copy.wait()


def own_half(*refs):
    sources, total, passed_on = refs[:11], refs[11], refs[12:16]
    held, rights, arrived, leaving, scratch = refs[16:27], refs[27:31], refs[31], refs[32], refs[33:]
    copies = [pltpu.make_async_copy(source, to, arrived.at[n]) for n, (source, to) in enumerate(zip(sources, held))]
    for copy in copies:
        copy.start()
    copies[0].wait()
    copy_places(held[0], scratch[0], scratch[1])
    onward = [
        pltpu.make_async_copy(source.at[pl.ds(HALF_ROWS, HALF_ROWS)], to, leaving.at[n])
        for n, (source, to) in enumerate(zip(rights, passed_on))
    ]

    def ready(family):
        pieces = slice(5 * family + 1, 5 * family + 6)
        for copy in copies[pieces]:
            copy.wait()
        prepare_right(held[pieces], family == 0, *rights[2 * family:2 * family + 2])
        for copy in onward[2 * family:2 * family + 2]:
            copy.start()

    total[...] = multiply(held[0], rights, ready, *scratch)
    for copy in onward:
        copy.wait()


def other_half_of(*refs):
    c_filter, panel, before, sources, out = refs[0], refs[1], refs[2], refs[3:7], refs[7]
    rights, arrived, scratch = refs[8:12], refs[12], refs[13:]
    copies = [pltpu.make_async_copy(source, to, arrived.at[n]) for n, (source, to) in enumerate(zip(sources, rights))]
    for copy in copies:
        copy.start()
    copy_places(panel, scratch[0], scratch[1])

    def ready(family):
        for copy in copies[2 * family:2 * family + 2]:
            copy.wait()

    total = before[...] + multiply(panel, rights, ready, *scratch)
    for i in range(4):
        for j in range(4):
            value = total[i * BS:(i + 1) * BS, j * BS:(j + 1) * BS]
            out[i, j] = jnp.where(c_filter[i, j] > 0, value, 0.0)


VMEM = pl.BlockSpec(memory_space=pltpu.VMEM)
SMEM = pl.BlockSpec(memory_space=pltpu.SMEM)
ANY = pl.BlockSpec(memory_space=pl.ANY)


def on_device(a_blocks, b_blocks, a_occupied, b_occupied, c_filter, row_sizes, k_sizes, col_sizes):
    right = pl.pallas_call(
        mask_right,
        out_shape=jax.ShapeDtypeStruct((4 * BS, BS), jnp.float32),
        in_specs=[VMEM, SMEM, SMEM, SMEM],
        out_specs=VMEM,
    )(b_blocks, b_occupied, k_sizes, col_sizes)
    partner = send(right, other_half())
    left = pl.pallas_call(
        pack_left,
        out_shape=jax.ShapeDtypeStruct((PAY_ROWS, BS), jnp.float32),
        in_specs=[VMEM, SMEM, SMEM, SMEM],
        out_specs=VMEM,
    )(a_blocks, a_occupied, row_sizes, k_sizes)
    same_core = [[zl * NC + core for zl in range(NZL)] for core in range(NC)]
    own = lax.all_gather(left, "col", axis_index_groups=same_core, tiled=True)
    first = [right, *near(right, along_x)]
    second = [partner, *near(partner, along_y)]
    parts = lax.optimization_barrier((*first, *second))
    first, second = jnp.concatenate(parts[:4]), jnp.concatenate(parts[4:])
    rights = (first, *gather_far(first, along_y), second, *gather_far(second, along_x))
    own, *rights = lax.optimization_barrier((own, *rights))
    other = send(own, other_core())
    scratch = [
        pltpu.SMEM((NZL, 8, BS), jnp.float32),
        pltpu.SemaphoreType.DMA((NZL,)),
        pltpu.VMEM((4 * BS, 16 * BS), jnp.bfloat16),
        pltpu.VMEM((4 * BS, 16 * BS), jnp.bfloat16),
    ]
    cost = pl.CostEstimate(flops=6 * 512 * 512 * 2048, bytes_accessed=8 << 20, transcendentals=0)
    part, *prepared = pl.pallas_call(
        own_half,
        out_shape=[jax.ShapeDtypeStruct((4 * BS, 4 * BS), jnp.float32)]
        + [jax.ShapeDtypeStruct((HALF_ROWS, 4 * BS), jnp.bfloat16)] * 4,
        in_specs=[ANY] * 11,
        out_specs=[VMEM] + [ANY] * 4,
        scratch_shapes=[pltpu.VMEM(source.shape, jnp.float32) for source in (own, *rights)]
        + [pltpu.VMEM((2 * HALF_ROWS, 4 * BS), jnp.bfloat16)] * 4
        + [pltpu.SemaphoreType.DMA((11,)), pltpu.SemaphoreType.DMA((4,))]
        + scratch,
        compiler_params=pltpu.CompilerParams(vmem_limit_bytes=46 << 20),
        cost_estimate=cost,
    )(own, *rights)
    return pl.pallas_call(
        other_half_of,
        out_shape=jax.ShapeDtypeStruct((4, 4, BS, BS), jnp.float32),
        in_specs=[SMEM] + [VMEM] * 2 + [ANY] * 4,
        out_specs=VMEM,
        scratch_shapes=[pltpu.VMEM((HALF_ROWS, 4 * BS), jnp.bfloat16)] * 4 + [pltpu.SemaphoreType.DMA((4,))] + scratch,
        compiler_params=pltpu.CompilerParams(vmem_limit_bytes=24 << 20),
        cost_estimate=cost,
    )(c_filter, other, part, *prepared)


def solution(mesh):
    placed = (
        P("row", "col", None, None),
        P("row", "col", None, None),
        P("row", "col"),
        P("row", "col"),
        P("row", "col"),
        P("row"),
        P(),
        P("col"),
    )
    return jax.shard_map(
        on_device,
        mesh=mesh,
        in_specs=placed,
        out_specs=P("row", "col", None, None),
        check_vma=False,
    )
```

```python
import functools

import jax
import jax.numpy as jnp
from jax import lax
from jax.experimental import pallas as pl
from jax.experimental.pallas import tpu as pltpu
from jax.sharding import PartitionSpec as P

BS = 128
CAP = 6
SLOT_ROWS = CAP * BS
PAY_ROWS = SLOT_ROWS + 8
HALF_ROWS = 8 * BS
AXES = ("row", "col")
NX, NY, NZH, NZL, NC = 4, 4, 2, 8, 2


def device_pairs(move):
    pairs = []
    for zh in range(NZH):
        for x in range(NX):
            for y in range(NY):
                for zl in range(NZL):
                    for core in range(NC):
                        to = move(zh, x, y, zl, core)
                        pairs.append((linear(zh, x, y, zl, core), linear(*to)))
    return pairs


def linear(zh, x, y, zl, core):
    return (((zh * NX + x) * NY + y) * NZL + zl) * NC + core


def along_x(n):
    return device_pairs(lambda zh, x, y, zl, core: (zh, (x + n) % NX, y, zl, core))


def along_y(n):
    return device_pairs(lambda zh, x, y, zl, core: (zh, x, (y + n) % NY, zl, core))


def other_half():
    return device_pairs(lambda zh, x, y, zl, core: (1 - zh, x, y, zl, core))


def other_core():
    return device_pairs(lambda zh, x, y, zl, core: (zh, x, y, zl, 1 - core))


def send(value, pairs):
    return lax.ppermute(value, AXES, pairs)


def near(block, along):
    return send(block, along(1)), send(block, along(-1)), send(block, along(2))


def gather_far(group, along):
    half = group.shape[0] // 2
    below = send(group, along(1))
    above = send(group, along(-1))
    return below, above, send(below[:half], along(1)), send(above[half:], along(-1))


def pack_left(blocks, occupied, row_sizes, k_sizes, out):
    first_k = lax.axis_index("col") * 2
    line = lax.broadcasted_iota(jnp.int32, (BS, BS), 0)
    lane = lax.broadcasted_iota(jnp.int32, (BS, BS), 1)
    slot = jnp.int32(0)
    for i in range(4):
        for k in range(2):
            here = (occupied[i, k] > 0) & (slot < CAP)
            place = slot

            @pl.when(here)
            def _():
                keep = (line < row_sizes[i]) & (lane < k_sizes[first_k + k])
                start = pl.multiple_of(place * BS, BS)
                out[pl.ds(start, BS), :] = jnp.where(keep, blocks[i, k], 0.0)

            where = jnp.where(here, place, -1).astype(jnp.float32)
            out[SLOT_ROWS + 2 * i + k, :] = jnp.full((BS,), where, jnp.float32)
            slot = slot + here.astype(jnp.int32)


def mask_right(blocks, occupied, k_sizes, col_sizes, out):
    used = k_sizes[lax.axis_index("row")]
    line = lax.broadcasted_iota(jnp.int32, (BS, BS), 0)
    lane = lax.broadcasted_iota(jnp.int32, (BS, BS), 1)
    for j in range(4):
        columns = jnp.where(occupied[0, j] > 0, col_sizes[j], 0)
        out[j * BS:(j + 1) * BS, :] = jnp.where((line < used) & (lane < columns), blocks[0, j], 0.0)


def split(value):
    high = value.astype(jnp.bfloat16)
    return high, (value - high.astype(jnp.float32)).astype(jnp.bfloat16)


NEAR = (0, -1, 1, 2)


def prepare_right(own_family, *refs):
    pieces, outs = refs[:5], refs[5:]
    row, core = lax.axis_index("row"), lax.axis_index("col") % 2
    x, y = (row // 4) % 4, row % 4
    for step in range(4):
        for t in range(4):
            ref, at = (pieces[step], t) if step < 3 else (pieces[3 + t // 2], t % 2)
            across, along = (NEAR[t], NEAR[step]) if own_family else (NEAR[step], NEAR[t])
            from_x, from_y = (x + across + 4) % 4, (y + along + 4) % 4
            foreign = from_y // 2 != core
            start = pl.multiple_of(from_x * 2 * BS + from_y % 2 * BS, BS)
            for other in range(2):

                @pl.when(foreign if other else jnp.logical_not(foreign))
                def _():
                    for j in range(4):
                        high, low = split(ref[(4 * at + j) * BS:(4 * at + j + 1) * BS, :])
                        outs[2 * other][pl.ds(start, BS), j * BS:(j + 1) * BS] = high
                        outs[2 * other + 1][pl.ds(start, BS), j * BS:(j + 1) * BS] = low


def multiply(last, *refs):
    if last:
        c_filter, panel, before = refs[:3]
        refs = refs[3:]
    else:
        panel, refs = refs[0], refs[1:]
    sources, out, rights, arrived, refs = refs[:4], refs[4], refs[5:9], refs[9], refs[10:]
    if not last:
        held, landed, refs = refs[0], refs[1], refs[2:]
    places, copied, left_high, left_low = refs
    zh = lax.axis_index("row") // 16
    copies = [
        pltpu.make_async_copy(source, to, arrived.at[n])
        for n, (source, to) in enumerate(zip(sources, rights))
    ]
    if not last:
        loading = pltpu.make_async_copy(panel, held, landed)
        loading.start()
    for copy in copies:
        copy.start()
    if not last:
        loading.wait()
        panel = held
    placing = [
        pltpu.make_async_copy(panel.at[pl.ds(zl * PAY_ROWS + SLOT_ROWS, 8)], places.at[zl], copied.at[zl])
        for zl in range(NZL)
    ]
    for copy in placing:
        copy.start()
    for copy in placing:
        copy.wait()

    def unpack(n):
        zl = (zh if n < 4 else 1 - zh) * 4 + n % 4
        for i in range(4):
            for k in range(2):
                slot = places[zl, 2 * i + k, 0].astype(jnp.int32)
                start = pl.multiple_of(zl * PAY_ROWS + jnp.maximum(slot, 0) * BS, 8)
                high, low = split(jnp.where(slot >= 0, panel[pl.ds(start, BS), :], 0.0))
                left_high[i * BS:(i + 1) * BS, (2 * n + k) * BS:(2 * n + k + 1) * BS] = high
                left_low[i * BS:(i + 1) * BS, (2 * n + k) * BS:(2 * n + k + 1) * BS] = low

    dot = functools.partial(jnp.dot, preferred_element_type=jnp.float32)
    total = before[...] if last else None
    for n in range(4):
        unpack(n)
    for family in range(2):
        if family == 0:
            for n in range(4, 8):
                unpack(n)
        for copy in copies[2 * family:2 * family + 2]:
            copy.wait()
        wide = slice(HALF_ROWS * family, HALF_ROWS * (family + 1))
        right_high, right_low = rights[2 * family][...], rights[2 * family + 1][...]
        part = dot(left_high[:, wide], right_high)
        part = part + dot(left_high[:, wide], right_low)
        part = part + dot(left_low[:, wide], right_high)
        total = part if total is None else total + part
    if not last:
        out[...] = total
        return
    for i in range(4):
        for j in range(4):
            value = total[i * BS:(i + 1) * BS, j * BS:(j + 1) * BS]
            out[i, j] = jnp.where(c_filter[i, j] > 0, value, 0.0)


VMEM = pl.BlockSpec(memory_space=pltpu.VMEM)
SMEM = pl.BlockSpec(memory_space=pltpu.SMEM)
ANY = pl.BlockSpec(memory_space=pl.ANY)


def on_device(a_blocks, b_blocks, a_occupied, b_occupied, c_filter, row_sizes, k_sizes, col_sizes):
    right = pl.pallas_call(
        mask_right,
        out_shape=jax.ShapeDtypeStruct((4 * BS, BS), jnp.float32),
        in_specs=[VMEM, SMEM, SMEM, SMEM],
        out_specs=VMEM,
    )(b_blocks, b_occupied, k_sizes, col_sizes)
    partner = send(right, other_half())
    first = [right, *near(right, along_x)]
    left = pl.pallas_call(
        pack_left,
        out_shape=jax.ShapeDtypeStruct((PAY_ROWS, BS), jnp.float32),
        in_specs=[VMEM, SMEM, SMEM, SMEM],
        out_specs=VMEM,
    )(a_blocks, a_occupied, row_sizes, k_sizes)
    same_core = [[zl * NC + core for zl in range(NZL)] for core in range(NC)]
    own = lax.all_gather(left, "col", axis_index_groups=same_core, tiled=True)
    partner, *first = lax.optimization_barrier((partner, *first))
    second = [partner, *near(partner, along_y)]
    first = jnp.concatenate(first)
    second = jnp.concatenate(lax.optimization_barrier(tuple(second)))
    rights = (first, *gather_far(first, along_y), second, *gather_far(second, along_x))
    prepared = []
    for family in range(2):
        prepared += pl.pallas_call(
            functools.partial(prepare_right, family == 0),
            out_shape=[jax.ShapeDtypeStruct((HALF_ROWS, 4 * BS), jnp.bfloat16)] * 4,
            in_specs=[VMEM] * 5,
            out_specs=[VMEM] * 4,
            compiler_params=pltpu.CompilerParams(vmem_limit_bytes=24 << 20),
        )(*rights[5 * family:5 * family + 5])
    own, *prepared = lax.optimization_barrier((own, *prepared))
    other = send(own, other_core())
    gathered = [pltpu.VMEM((HALF_ROWS, 4 * BS), jnp.bfloat16)] * 4 + [pltpu.SemaphoreType.DMA((4,))]
    scratch = [
        pltpu.SMEM((NZL, 8, BS), jnp.float32),
        pltpu.SemaphoreType.DMA((NZL,)),
        pltpu.VMEM((4 * BS, 16 * BS), jnp.bfloat16),
        pltpu.VMEM((4 * BS, 16 * BS), jnp.bfloat16),
    ]
    cost = pl.CostEstimate(flops=6 * 512 * 512 * 2048, bytes_accessed=8 << 20, transcendentals=0)
    part = pl.pallas_call(
        functools.partial(multiply, False),
        out_shape=jax.ShapeDtypeStruct((4 * BS, 4 * BS), jnp.float32),
        in_specs=[ANY] * 5,
        out_specs=VMEM,
        scratch_shapes=gathered
        + [pltpu.VMEM((NZL * PAY_ROWS, BS), jnp.float32), pltpu.SemaphoreType.DMA]
        + scratch,
        compiler_params=pltpu.CompilerParams(vmem_limit_bytes=52 << 20),
        cost_estimate=cost,
    )(own, *prepared[:2], *prepared[4:6])
    return pl.pallas_call(
        functools.partial(multiply, True),
        out_shape=jax.ShapeDtypeStruct((4, 4, BS, BS), jnp.float32),
        in_specs=[SMEM] + [VMEM] * 2 + [ANY] * 4,
        out_specs=VMEM,
        scratch_shapes=gathered + scratch,
        compiler_params=pltpu.CompilerParams(vmem_limit_bytes=24 << 20),
        cost_estimate=cost,
    )(c_filter, other, part, *prepared[2:4], *prepared[6:])


def solution(mesh):
    placed = (
        P("row", "col", None, None),
        P("row", "col", None, None),
        P("row", "col"),
        P("row", "col"),
        P("row", "col"),
        P("row"),
        P(),
        P("col"),
    )
    return jax.shard_map(
        on_device,
        mesh=mesh,
        in_specs=placed,
        out_specs=P("row", "col", None, None),
        check_vma=False,
    )
```

```python
import functools

import jax
import jax.numpy as jnp
from jax import lax
from jax.experimental import pallas as pl
from jax.experimental.pallas import tpu as pltpu
from jax.sharding import PartitionSpec as P

BS = 128
CAP = 6
SLOT_ROWS = CAP * BS
PAY_ROWS = SLOT_ROWS + 8
HALF_ROWS = 8 * BS
AXES = ("row", "col")
NX, NY, NZH, NZL, NC = 4, 4, 2, 8, 2


def device_pairs(move):
    pairs = []
    for zh in range(NZH):
        for x in range(NX):
            for y in range(NY):
                for zl in range(NZL):
                    for core in range(NC):
                        to = move(zh, x, y, zl, core)
                        pairs.append((linear(zh, x, y, zl, core), linear(*to)))
    return pairs


def linear(zh, x, y, zl, core):
    return (((zh * NX + x) * NY + y) * NZL + zl) * NC + core


def along_x(n):
    return device_pairs(lambda zh, x, y, zl, core: (zh, (x + n) % NX, y, zl, core))


def along_y(n):
    return device_pairs(lambda zh, x, y, zl, core: (zh, x, (y + n) % NY, zl, core))


def other_half():
    return device_pairs(lambda zh, x, y, zl, core: (1 - zh, x, y, zl, core))


def other_core():
    return device_pairs(lambda zh, x, y, zl, core: (zh, x, y, zl, 1 - core))


def send(value, pairs):
    return lax.ppermute(value, AXES, pairs)


def near(block, along):
    return send(block, along(1)), send(block, along(-1)), send(block, along(2))


def gather_far(group, along):
    half = group.shape[0] // 2
    below = send(group, along(1))
    above = send(group, along(-1))
    return below, above, send(below[:half], along(1)), send(above[half:], along(-1))


def pack_left(blocks, occupied, row_sizes, k_sizes, out):
    first_k = lax.axis_index("col") * 2
    line = lax.broadcasted_iota(jnp.int32, (BS, BS), 0)
    lane = lax.broadcasted_iota(jnp.int32, (BS, BS), 1)
    slot = jnp.int32(0)
    for i in range(4):
        for k in range(2):
            here = (occupied[i, k] > 0) & (slot < CAP)
            place = slot

            @pl.when(here)
            def _():
                keep = (line < row_sizes[i]) & (lane < k_sizes[first_k + k])
                start = pl.multiple_of(place * BS, BS)
                out[pl.ds(start, BS), :] = jnp.where(keep, blocks[i, k], 0.0)

            where = jnp.where(here, place, -1).astype(jnp.float32)
            out[SLOT_ROWS + 2 * i + k, :] = jnp.full((BS,), where, jnp.float32)
            slot = slot + here.astype(jnp.int32)


def mask_right(blocks, occupied, k_sizes, col_sizes, out):
    used = k_sizes[lax.axis_index("row")]
    line = lax.broadcasted_iota(jnp.int32, (BS, BS), 0)
    lane = lax.broadcasted_iota(jnp.int32, (BS, BS), 1)
    for j in range(4):
        columns = jnp.where(occupied[0, j] > 0, col_sizes[j], 0)
        out[j * BS:(j + 1) * BS, :] = jnp.where((line < used) & (lane < columns), blocks[0, j], 0.0)


def split(value):
    high = value.astype(jnp.bfloat16)
    return high, (value - high.astype(jnp.float32)).astype(jnp.bfloat16)


NEAR = (0, -1, 1, 2)


def prepare_right(along_first, *refs):
    pieces, outs = refs[:5], refs[5:]
    wide = outs[0].shape[1] // BS
    row, core = lax.axis_index("row"), lax.axis_index("col") % 2
    x, y = (row // 4) % 4, row % 4
    for step in range(4):
        for t in range(4):
            ref, at = (pieces[step], t) if step < 3 else (pieces[3 + t // 2], t % 2)
            across, along = (NEAR[t], NEAR[step]) if along_first == "x" else (NEAR[step], NEAR[t])
            from_x, from_y = (x + across + 4) % 4, (y + along + 4) % 4
            foreign = from_y // 2 != core
            start = pl.multiple_of(from_x * 2 * BS + from_y % 2 * BS, BS)
            for other in range(2):

                @pl.when(foreign if other else jnp.logical_not(foreign))
                def _():
                    for j in range(wide):
                        high, low = split(ref[(wide * at + j) * BS:(wide * at + j + 1) * BS, :])
                        outs[2 * other][pl.ds(start, BS), j * BS:(j + 1) * BS] = high
                        outs[2 * other + 1][pl.ds(start, BS), j * BS:(j + 1) * BS] = low


def multiply(families, first, last, *refs):
    many = 2 * len(families)
    refs = list(refs)
    c_filter = refs.pop(0) if last else None
    before = None if first else refs.pop(0)
    source, sources, out = refs[0], refs[1:1 + many], refs[1 + many]
    held, rights, arrived, places, copied, left_high, left_low = refs[2 + many], refs[3 + many:3 + 2 * many], *refs[3 + 2 * many:]
    zh = lax.axis_index("row") // 16
    loading, placing = [], []
    for at in range(4 * len(families)):
        family = families[at // 4]
        zl = (1 - zh if family else zh) * 4 + at % 4
        start = pl.multiple_of(zl * PAY_ROWS, 8)
        here = slice(at * PAY_ROWS, (at + 1) * PAY_ROWS)
        loading.append(pltpu.make_async_copy(source.at[pl.ds(start, PAY_ROWS)], held.at[here], arrived.at[at]))
        ends = slice(at * PAY_ROWS + SLOT_ROWS, (at + 1) * PAY_ROWS)
        placing.append(pltpu.make_async_copy(held.at[ends], places.at[at], copied.at[at]))
    copies = [pltpu.make_async_copy(begin, to, arrived.at[8 + n]) for n, (begin, to) in enumerate(zip(sources, rights))]
    for copy in loading + copies:
        copy.start()
    for copy, place in zip(loading, placing):
        copy.wait()
        place.start()
    for place in placing:
        place.wait()
    for at in range(4 * len(families)):
        for i in range(4):
            for k in range(2):
                slot = places[at, 2 * i + k, 0].astype(jnp.int32)
                start = pl.multiple_of(at * PAY_ROWS + jnp.maximum(slot, 0) * BS, 8)
                high, low = split(jnp.where(slot >= 0, held[pl.ds(start, BS), :], 0.0))
                left_high[i * BS:(i + 1) * BS, (2 * at + k) * BS:(2 * at + k + 1) * BS] = high
                left_low[i * BS:(i + 1) * BS, (2 * at + k) * BS:(2 * at + k + 1) * BS] = low
    dot = functools.partial(jnp.dot, preferred_element_type=jnp.float32)
    total = None if first else before[...]
    for n in range(len(families)):
        wide = slice(HALF_ROWS * n, HALF_ROWS * (n + 1))
        for copy in copies[2 * n:2 * n + 2]:
            copy.wait()
        right_high, right_low = rights[2 * n][...], rights[2 * n + 1][...]
        part = dot(left_high[:, wide], right_high) + dot(left_high[:, wide], right_low)
        part = part + dot(left_low[:, wide], right_high)
        total = part if total is None else total + part
    if not last:
        out[...] = total
        return
    for i in range(4):
        for j in range(4):
            value = total[i * BS:(i + 1) * BS, j * BS:(j + 1) * BS]
            out[i, j] = jnp.where(c_filter[i, j] > 0, value, 0.0)


def add_products(families, panel, rights, before=None, c_filter=None, limit=52, flops=1 << 30):
    last = c_filter is not None
    operands = ([c_filter] if last else []) + ([] if before is None else [before]) + [panel, *rights]
    specs = ([SMEM] if last else []) + ([] if before is None else [VMEM]) + [ANY] * (1 + len(rights))
    count = len(families)
    shape = (4, 4, BS, BS) if last else (4 * BS, 4 * BS)
    return pl.pallas_call(
        functools.partial(multiply, families, before is None, last),
        out_shape=jax.ShapeDtypeStruct(shape, jnp.float32),
        in_specs=specs,
        out_specs=VMEM,
        scratch_shapes=[pltpu.VMEM((4 * count * PAY_ROWS, BS), jnp.float32)]
        + [pltpu.VMEM(part.shape, part.dtype) for part in rights]
        + [
            pltpu.SemaphoreType.DMA((12,)),
            pltpu.SMEM((NZL, 8, BS), jnp.float32),
            pltpu.SemaphoreType.DMA((NZL,)),
            pltpu.VMEM((4 * BS, 8 * count * BS), jnp.bfloat16),
            pltpu.VMEM((4 * BS, 8 * count * BS), jnp.bfloat16),
        ],
        compiler_params=pltpu.CompilerParams(vmem_limit_bytes=limit << 20),
        cost_estimate=pl.CostEstimate(flops=flops, bytes_accessed=4 << 20, transcendentals=0),
    )(*operands)


VMEM = pl.BlockSpec(memory_space=pltpu.VMEM)
SMEM = pl.BlockSpec(memory_space=pltpu.SMEM)
ANY = pl.BlockSpec(memory_space=pl.ANY)


def prepare(pieces, along_first):
    return pl.pallas_call(
        functools.partial(prepare_right, along_first),
        out_shape=[jax.ShapeDtypeStruct((HALF_ROWS, 4 * BS), jnp.bfloat16)] * 4,
        in_specs=[VMEM] * 5,
        out_specs=[VMEM] * 4,
        compiler_params=pltpu.CompilerParams(vmem_limit_bytes=24 << 20),
    )(*pieces)


def on_device(a_blocks, b_blocks, a_occupied, b_occupied, c_filter, row_sizes, k_sizes, col_sizes):
    right = pl.pallas_call(
        mask_right,
        out_shape=jax.ShapeDtypeStruct((4 * BS, BS), jnp.float32),
        in_specs=[VMEM, SMEM, SMEM, SMEM],
        out_specs=VMEM,
    )(b_blocks, b_occupied, k_sizes, col_sizes)
    partner = send(right, other_half())
    first = [right, *near(right, along_x)]
    left = pl.pallas_call(
        pack_left,
        out_shape=jax.ShapeDtypeStruct((PAY_ROWS, BS), jnp.float32),
        in_specs=[VMEM, SMEM, SMEM, SMEM],
        out_specs=VMEM,
    )(a_blocks, a_occupied, row_sizes, k_sizes)
    same_core = [[zl * NC + core for zl in range(NZL)] for core in range(NC)]
    own = lax.all_gather(left, "col", axis_index_groups=same_core, tiled=True)
    partner, *first = lax.optimization_barrier((partner, *first))
    second = [partner, *near(partner, along_y)]
    first = jnp.concatenate(first)
    second = jnp.concatenate(lax.optimization_barrier(tuple(second)))
    first = [first, *gather_far(first, along_y)]
    second = [second, *gather_far(second, along_x)]
    near_by = prepare(first, "x")
    own, near_by, second[1], second[2] = lax.optimization_barrier((own, near_by, second[1], second[2]))
    other = send(own, other_core())
    far_off = prepare(second, "y")
    part = add_products((0,), own, near_by[:2], limit=52)
    part = add_products((1,), own, far_off[:2], before=part, limit=24, flops=80 << 30)
    return add_products((0, 1), other, (*near_by[2:], *far_off[2:]), before=part, c_filter=c_filter, limit=36)


def solution(mesh):
    placed = (
        P("row", "col", None, None),
        P("row", "col", None, None),
        P("row", "col"),
        P("row", "col"),
        P("row", "col"),
        P("row"),
        P(),
        P("col"),
    )
    return jax.shard_map(
        on_device,
        mesh=mesh,
        in_specs=placed,
        out_specs=P("row", "col", None, None),
        check_vma=False,
    )
```

```python
import functools

import jax
import jax.numpy as jnp
from jax import lax
from jax.experimental import pallas as pl
from jax.experimental.pallas import tpu as pltpu
from jax.sharding import PartitionSpec as P

BS = 128
CAP = 6
SLOT_ROWS = CAP * BS
PAY_ROWS = SLOT_ROWS + 8
HALF_ROWS = 8 * BS
AXES = ("row", "col")
NX, NY, NZH, NZL, NC = 4, 4, 2, 8, 2


def device_pairs(move):
    pairs = []
    for zh in range(NZH):
        for x in range(NX):
            for y in range(NY):
                for zl in range(NZL):
                    for core in range(NC):
                        to = move(zh, x, y, zl, core)
                        pairs.append((linear(zh, x, y, zl, core), linear(*to)))
    return pairs


def linear(zh, x, y, zl, core):
    return (((zh * NX + x) * NY + y) * NZL + zl) * NC + core


def along_x(n):
    return device_pairs(lambda zh, x, y, zl, core: (zh, (x + n) % NX, y, zl, core))


def along_y(n):
    return device_pairs(lambda zh, x, y, zl, core: (zh, x, (y + n) % NY, zl, core))


def other_half():
    return device_pairs(lambda zh, x, y, zl, core: (1 - zh, x, y, zl, core))


def other_core():
    return device_pairs(lambda zh, x, y, zl, core: (zh, x, y, zl, 1 - core))


def send(value, pairs):
    return lax.ppermute(value, AXES, pairs)


def near(block, along):
    return send(block, along(1)), send(block, along(-1)), send(block, along(2))


def gather_far(group, along):
    half = group.shape[0] // 2
    below = send(group, along(1))
    above = send(group, along(-1))
    return below, above, send(below[:half], along(1)), send(above[half:], along(-1))


def pack_left(blocks, occupied, row_sizes, k_sizes, out):
    first_k = lax.axis_index("col") * 2
    line = lax.broadcasted_iota(jnp.int32, (BS, BS), 0)
    lane = lax.broadcasted_iota(jnp.int32, (BS, BS), 1)
    slot = jnp.int32(0)
    for i in range(4):
        for k in range(2):
            here = (occupied[i, k] > 0) & (slot < CAP)
            place = slot

            @pl.when(here)
            def _():
                keep = (line < row_sizes[i]) & (lane < k_sizes[first_k + k])
                start = pl.multiple_of(place * BS, BS)
                out[pl.ds(start, BS), :] = jnp.where(keep, blocks[i, k], 0.0)

            where = jnp.where(here, place, -1).astype(jnp.float32)
            out[SLOT_ROWS + 2 * i + k, :] = jnp.full((BS,), where, jnp.float32)
            slot = slot + here.astype(jnp.int32)


def mask_right(blocks, occupied, k_sizes, col_sizes, out):
    used = k_sizes[lax.axis_index("row")]
    line = lax.broadcasted_iota(jnp.int32, (BS, BS), 0)
    lane = lax.broadcasted_iota(jnp.int32, (BS, BS), 1)
    for j in range(4):
        columns = jnp.where(occupied[0, j] > 0, col_sizes[j], 0)
        out[j * BS:(j + 1) * BS, :] = jnp.where((line < used) & (lane < columns), blocks[0, j], 0.0)


def split(value):
    high = value.astype(jnp.bfloat16)
    return high, (value - high.astype(jnp.float32)).astype(jnp.bfloat16)


NEAR = (0, -1, 1, 2)


def prepare_right(along_first, *refs):
    pieces, outs = refs[:5], refs[5:]
    wide = outs[0].shape[1] // BS
    row, core = lax.axis_index("row"), lax.axis_index("col") % 2
    x, y = (row // 4) % 4, row % 4
    for step in range(4):
        for t in range(4):
            ref, at = (pieces[step], t) if step < 3 else (pieces[3 + t // 2], t % 2)
            across, along = (NEAR[t], NEAR[step]) if along_first == "x" else (NEAR[step], NEAR[t])
            from_x, from_y = (x + across + 4) % 4, (y + along + 4) % 4
            foreign = from_y // 2 != core
            start = pl.multiple_of(from_x * 2 * BS + from_y % 2 * BS, BS)
            for other in range(2):

                @pl.when(foreign if other else jnp.logical_not(foreign))
                def _():
                    for j in range(wide):
                        high, low = split(ref[(wide * at + j) * BS:(wide * at + j + 1) * BS, :])
                        outs[2 * other][pl.ds(start, BS), j * BS:(j + 1) * BS] = high
                        outs[2 * other + 1][pl.ds(start, BS), j * BS:(j + 1) * BS] = low


def multiply(last, *refs):
    if last:
        c_filter, before, panel, *rights = refs[:7]
        out, places, copied, left_high, left_low = refs[7:]
    else:
        panel, *rights = refs[:5]
        out, places, copied, left_high, left_low = refs[5:]
    zh = lax.axis_index("row") // 16
    placing = [
        pltpu.make_async_copy(panel.at[pl.ds(zl * PAY_ROWS + SLOT_ROWS, 8)], places.at[zl], copied.at[zl])
        for zl in range(NZL)
    ]
    for copy in placing:
        copy.start()
    for copy in placing:
        copy.wait()
    for n in range(8):
        zl = (zh if n < 4 else 1 - zh) * 4 + n % 4
        for i in range(4):
            for k in range(2):
                slot = places[zl, 2 * i + k, 0].astype(jnp.int32)
                start = pl.multiple_of(zl * PAY_ROWS + jnp.maximum(slot, 0) * BS, 8)
                high, low = split(jnp.where(slot >= 0, panel[pl.ds(start, BS), :], 0.0))
                left_high[i * BS:(i + 1) * BS, (2 * n + k) * BS:(2 * n + k + 1) * BS] = high
                left_low[i * BS:(i + 1) * BS, (2 * n + k) * BS:(2 * n + k + 1) * BS] = low
    dot = functools.partial(jnp.dot, preferred_element_type=jnp.float32)
    total = before[...] if last else None
    for family in range(2):
        wide = slice(HALF_ROWS * family, HALF_ROWS * (family + 1))
        right_high, right_low = rights[2 * family][...], rights[2 * family + 1][...]
        part = dot(left_high[:, wide], right_high) + dot(left_high[:, wide], right_low)
        part = part + dot(left_low[:, wide], right_high)
        total = part if total is None else total + part
    if not last:
        out[...] = total
        return
    for i in range(4):
        for j in range(4):
            value = total[i * BS:(i + 1) * BS, j * BS:(j + 1) * BS]
            out[i, j] = jnp.where(c_filter[i, j] > 0, value, 0.0)


def add_products(panel, rights, before=None, c_filter=None, flops=1 << 30):
    last = c_filter is not None
    return pl.pallas_call(
        functools.partial(multiply, last),
        out_shape=jax.ShapeDtypeStruct((4, 4, BS, BS) if last else (4 * BS, 4 * BS), jnp.float32),
        in_specs=([SMEM, VMEM] if last else []) + [VMEM] * 5,
        out_specs=VMEM,
        scratch_shapes=[
            pltpu.SMEM((NZL, 8, BS), jnp.float32),
            pltpu.SemaphoreType.DMA((NZL,)),
            pltpu.VMEM((4 * BS, 16 * BS), jnp.bfloat16),
            pltpu.VMEM((4 * BS, 16 * BS), jnp.bfloat16),
        ],
        compiler_params=pltpu.CompilerParams(vmem_limit_bytes=24 << 20),
        cost_estimate=pl.CostEstimate(flops=flops, bytes_accessed=4 << 20, transcendentals=0),
    )(*((c_filter, before) if last else ()), panel, *rights)


VMEM = pl.BlockSpec(memory_space=pltpu.VMEM)
SMEM = pl.BlockSpec(memory_space=pltpu.SMEM)
ANY = pl.BlockSpec(memory_space=pl.ANY)


def prepare(pieces, along_first):
    return pl.pallas_call(
        functools.partial(prepare_right, along_first),
        out_shape=[jax.ShapeDtypeStruct((HALF_ROWS, 4 * BS), jnp.bfloat16)] * 4,
        in_specs=[VMEM] * 5,
        out_specs=[VMEM] * 4,
        compiler_params=pltpu.CompilerParams(vmem_limit_bytes=24 << 20),
    )(*pieces)


def on_device(a_blocks, b_blocks, a_occupied, b_occupied, c_filter, row_sizes, k_sizes, col_sizes):
    right = pl.pallas_call(
        mask_right,
        out_shape=jax.ShapeDtypeStruct((4 * BS, BS), jnp.float32),
        in_specs=[VMEM, SMEM, SMEM, SMEM],
        out_specs=VMEM,
    )(b_blocks, b_occupied, k_sizes, col_sizes)
    first = [right, *near(right, along_x)]
    partner = send(right, other_half())
    left = pl.pallas_call(
        pack_left,
        out_shape=jax.ShapeDtypeStruct((PAY_ROWS, BS), jnp.float32),
        in_specs=[VMEM, SMEM, SMEM, SMEM],
        out_specs=VMEM,
    )(a_blocks, a_occupied, row_sizes, k_sizes)
    same_core = [[zl * NC + core for zl in range(NZL)] for core in range(NC)]
    own = lax.all_gather(left, "col", axis_index_groups=same_core, tiled=True)
    *first, partner = lax.optimization_barrier((*first, partner))
    second = [partner, *near(partner, along_y)]
    first = jnp.concatenate(first)
    second = jnp.concatenate(lax.optimization_barrier(tuple(second)))
    first = [first, *gather_far(first, along_y)]
    second = [second, *gather_far(second, along_x)]
    own, second[1], second[2] = lax.optimization_barrier((own, second[1], second[2]))
    other = send(own, other_core())
    near_by, far_off = prepare(first, "x"), prepare(second, "y")
    part = add_products(own, (*near_by[:2], *far_off[:2]), flops=30 << 30)
    return add_products(other, (*near_by[2:], *far_off[2:]), before=part, c_filter=c_filter)


def solution(mesh):
    placed = (
        P("row", "col", None, None),
        P("row", "col", None, None),
        P("row", "col"),
        P("row", "col"),
        P("row", "col"),
        P("row"),
        P(),
        P("col"),
    )
    return jax.shard_map(
        on_device,
        mesh=mesh,
        in_specs=placed,
        out_specs=P("row", "col", None, None),
        check_vma=False,
    )
```

```python
import functools

import jax
import jax.numpy as jnp
from jax import lax
from jax.experimental import pallas as pl
from jax.experimental.pallas import tpu as pltpu
from jax.sharding import PartitionSpec as P

BS = 128
CAP = 6
SLOT_ROWS = CAP * BS
PAY_ROWS = SLOT_ROWS + 8
HALF_ROWS = 8 * BS
AXES = ("row", "col")
NX, NY, NZH, NZL, NC = 4, 4, 2, 8, 2


def device_pairs(move):
    pairs = []
    for zh in range(NZH):
        for x in range(NX):
            for y in range(NY):
                for zl in range(NZL):
                    for core in range(NC):
                        to = move(zh, x, y, zl, core)
                        pairs.append((linear(zh, x, y, zl, core), linear(*to)))
    return pairs


def linear(zh, x, y, zl, core):
    return (((zh * NX + x) * NY + y) * NZL + zl) * NC + core


def along_x(n):
    return device_pairs(lambda zh, x, y, zl, core: (zh, (x + n) % NX, y, zl, core))


def along_y(n):
    return device_pairs(lambda zh, x, y, zl, core: (zh, x, (y + n) % NY, zl, core))


def other_half():
    return device_pairs(lambda zh, x, y, zl, core: (1 - zh, x, y, zl, core))


def other_core():
    return device_pairs(lambda zh, x, y, zl, core: (zh, x, y, zl, 1 - core))


def send(value, pairs):
    return lax.ppermute(value, AXES, pairs)


def near(block, along):
    return send(block, along(1)), send(block, along(-1)), send(block, along(2))


def gather_far(group, along):
    half = group.shape[0] // 2
    below = send(group, along(1))
    above = send(group, along(-1))
    return below, above, send(below[:half], along(1)), send(above[half:], along(-1))


def pack_left(blocks, occupied, row_sizes, k_sizes, out):
    first_k = lax.axis_index("col") * 2
    line = lax.broadcasted_iota(jnp.int32, (BS, BS), 0)
    lane = lax.broadcasted_iota(jnp.int32, (BS, BS), 1)
    slot = jnp.int32(0)
    for i in range(4):
        for k in range(2):
            here = (occupied[i, k] > 0) & (slot < CAP)
            place = slot

            @pl.when(here)
            def _():
                keep = (line < row_sizes[i]) & (lane < k_sizes[first_k + k])
                start = pl.multiple_of(place * BS, BS)
                out[pl.ds(start, BS), :] = jnp.where(keep, blocks[i, k], 0.0)

            where = jnp.where(here, place, -1).astype(jnp.float32)
            out[SLOT_ROWS + 2 * i + k, :] = jnp.full((BS,), where, jnp.float32)
            slot = slot + here.astype(jnp.int32)


def mask_right(blocks, occupied, k_sizes, col_sizes, out):
    used = k_sizes[lax.axis_index("row")]
    line = lax.broadcasted_iota(jnp.int32, (BS, BS), 0)
    lane = lax.broadcasted_iota(jnp.int32, (BS, BS), 1)
    for j in range(4):
        columns = jnp.where(occupied[0, j] > 0, col_sizes[j], 0)
        out[j * BS:(j + 1) * BS, :] = jnp.where((line < used) & (lane < columns), blocks[0, j], 0.0)


def split(value):
    high = value.astype(jnp.bfloat16)
    return high, (value - high.astype(jnp.float32)).astype(jnp.bfloat16)


NEAR = (0, -1, 1, 2)


def prepare_right(along_first, *refs):
    *pieces, high_out, low_out = refs
    row, core = lax.axis_index("row"), lax.axis_index("col") % 2
    x, y = (row // 4) % 4, row % 4
    for step in range(4):
        for t in range(4):
            whole = step < 3 or len(pieces) == 4
            ref, at = (pieces[step], t) if whole else (pieces[3 + t // 2], t % 2)
            across, along = (NEAR[t], NEAR[step]) if along_first == "x" else (NEAR[step], NEAR[t])
            from_x, from_y = (x + across + 4) % 4, (y + along + 4) % 4
            foreign = (from_y // 2 != core).astype(jnp.int32)
            start = pl.multiple_of(foreign * HALF_ROWS + from_x * 2 * BS + from_y % 2 * BS, BS)
            for j in range(4):
                high, low = split(ref[(4 * at + j) * BS:(4 * at + j + 1) * BS, :])
                high_out[pl.ds(start, BS), j * BS:(j + 1) * BS] = high
                low_out[pl.ds(start, BS), j * BS:(j + 1) * BS] = low


def multiply(families, first, last, *refs):
    refs = list(refs)
    c_filter = refs.pop(0) if last else None
    before = None if first else refs.pop(0)
    panel, *rights = refs[:-5]
    out, places, copied, left_high, left_low = refs[-5:]
    zh = lax.axis_index("row") // 16
    placing = [
        pltpu.make_async_copy(panel.at[pl.ds(zl * PAY_ROWS + SLOT_ROWS, 8)], places.at[zl], copied.at[zl])
        for zl in range(NZL)
    ]
    for copy in placing:
        copy.start()
    for copy in placing:
        copy.wait()
    for n in range(4 * len(families)):
        zl = (1 - zh if families[n // 4] else zh) * 4 + n % 4
        for i in range(4):
            for k in range(2):
                slot = places[zl, 2 * i + k, 0].astype(jnp.int32)
                start = pl.multiple_of(zl * PAY_ROWS + jnp.maximum(slot, 0) * BS, 8)
                high, low = split(jnp.where(slot >= 0, panel[pl.ds(start, BS), :], 0.0))
                left_high[i * BS:(i + 1) * BS, (2 * n + k) * BS:(2 * n + k + 1) * BS] = high
                left_low[i * BS:(i + 1) * BS, (2 * n + k) * BS:(2 * n + k + 1) * BS] = low
    dot = functools.partial(jnp.dot, preferred_element_type=jnp.float32)
    total = None if first else before[...]
    for family in range(len(families)):
        wide = slice(HALF_ROWS * family, HALF_ROWS * (family + 1))
        deep = slice(HALF_ROWS, 2 * HALF_ROWS) if last else slice(0, HALF_ROWS)
        right_high, right_low = rights[2 * family][deep, :], rights[2 * family + 1][deep, :]
        part = dot(left_high[:, wide], right_high) + dot(left_high[:, wide], right_low)
        part = part + dot(left_low[:, wide], right_high)
        total = part if total is None else total + part
    if not last:
        out[...] = total
        return
    for i in range(4):
        for j in range(4):
            value = total[i * BS:(i + 1) * BS, j * BS:(j + 1) * BS]
            out[i, j] = jnp.where(c_filter[i, j] > 0, value, 0.0)


def add_products(families, panel, rights, before=None, c_filter=None, flops=1 << 30):
    last, first = c_filter is not None, before is None
    return pl.pallas_call(
        functools.partial(multiply, families, first, last),
        out_shape=jax.ShapeDtypeStruct((4, 4, BS, BS) if last else (4 * BS, 4 * BS), jnp.float32),
        in_specs=([SMEM] if last else []) + ([] if first else [VMEM]) + [VMEM] * (1 + len(rights)),
        out_specs=VMEM,
        scratch_shapes=[
            pltpu.SMEM((NZL, 8, BS), jnp.float32),
            pltpu.SemaphoreType.DMA((NZL,)),
            pltpu.VMEM((4 * BS, 8 * len(families) * BS), jnp.bfloat16),
            pltpu.VMEM((4 * BS, 8 * len(families) * BS), jnp.bfloat16),
        ],
        compiler_params=pltpu.CompilerParams(vmem_limit_bytes=24 << 20),
        cost_estimate=pl.CostEstimate(flops=flops, bytes_accessed=4 << 20, transcendentals=0),
    )(*((c_filter,) if last else ()), *(() if first else (before,)), panel, *rights)


VMEM = pl.BlockSpec(memory_space=pltpu.VMEM)
SMEM = pl.BlockSpec(memory_space=pltpu.SMEM)


def prepare(pieces, along_first):
    return pl.pallas_call(
        functools.partial(prepare_right, along_first),
        out_shape=[jax.ShapeDtypeStruct((2 * HALF_ROWS, 4 * BS), jnp.bfloat16)] * 2,
        in_specs=[VMEM] * len(pieces),
        out_specs=[VMEM] * 2,
        compiler_params=pltpu.CompilerParams(vmem_limit_bytes=24 << 20),
    )(*pieces)


def on_device(a_blocks, b_blocks, a_occupied, b_occupied, c_filter, row_sizes, k_sizes, col_sizes):
    right = pl.pallas_call(
        mask_right,
        out_shape=jax.ShapeDtypeStruct((4 * BS, BS), jnp.float32),
        in_specs=[VMEM, SMEM, SMEM, SMEM],
        out_specs=VMEM,
    )(b_blocks, b_occupied, k_sizes, col_sizes)
    first = [right, *near(right, along_x)]
    partner = send(right, other_half())
    left = pl.pallas_call(
        pack_left,
        out_shape=jax.ShapeDtypeStruct((PAY_ROWS, BS), jnp.float32),
        in_specs=[VMEM, SMEM, SMEM, SMEM],
        out_specs=VMEM,
    )(a_blocks, a_occupied, row_sizes, k_sizes)
    same_core = [[zl * NC + core for zl in range(NZL)] for core in range(NC)]
    own = lax.all_gather(left, "col", axis_index_groups=same_core, tiled=True)
    *first, partner = lax.optimization_barrier((*first, partner))
    second = [partner, *near(partner, along_y)]
    first = jnp.concatenate(first)
    second = jnp.concatenate(lax.optimization_barrier(tuple(second)))
    first = [first, *near(first, along_y)]
    second = [second, *gather_far(second, along_x)]
    own, second[1], second[2] = lax.optimization_barrier((own, second[1], second[2]))
    other = send(own, other_core())
    near_by, far_off = prepare(first, "x"), prepare(second, "y")
    part = add_products((0, 1), own, (*near_by, *far_off), flops=30 << 30)
    return add_products((0, 1), other, (*near_by, *far_off), before=part, c_filter=c_filter)


def solution(mesh):
    placed = (
        P("row", "col", None, None),
        P("row", "col", None, None),
        P("row", "col"),
        P("row", "col"),
        P("row", "col"),
        P("row"),
        P(),
        P("col"),
    )
    return jax.shard_map(
        on_device,
        mesh=mesh,
        in_specs=placed,
        out_specs=P("row", "col", None, None),
        check_vma=False,
    )
```

```python
import functools

import jax
import jax.numpy as jnp
from jax import lax
from jax.experimental import pallas as pl
from jax.experimental.pallas import tpu as pltpu
from jax.sharding import PartitionSpec as P

BS = 128
CAP = 6
SLOT_ROWS = CAP * BS
PAY_ROWS = SLOT_ROWS + 8
HALF_ROWS = 8 * BS
AXES = ("row", "col")
NX, NY, NZH, NZL, NC = 4, 4, 2, 8, 2


def device_pairs(move):
    pairs = []
    for zh in range(NZH):
        for x in range(NX):
            for y in range(NY):
                for zl in range(NZL):
                    for core in range(NC):
                        to = move(zh, x, y, zl, core)
                        pairs.append((linear(zh, x, y, zl, core), linear(*to)))
    return pairs


def linear(zh, x, y, zl, core):
    return (((zh * NX + x) * NY + y) * NZL + zl) * NC + core


def along_x(n):
    return device_pairs(lambda zh, x, y, zl, core: (zh, (x + n) % NX, y, zl, core))


def along_y(n):
    return device_pairs(lambda zh, x, y, zl, core: (zh, x, (y + n) % NY, zl, core))


def other_half():
    return device_pairs(lambda zh, x, y, zl, core: (1 - zh, x, y, zl, core))


def other_core():
    return device_pairs(lambda zh, x, y, zl, core: (zh, x, y, zl, 1 - core))


def send(value, pairs):
    return lax.ppermute(value, AXES, pairs)


def near(block, along):
    return send(block, along(1)), send(block, along(-1)), send(block, along(2))


def gather_far(group, along):
    half = group.shape[0] // 2
    below = send(group, along(1))
    above = send(group, along(-1))
    return below, above, send(below[:half], along(1)), send(above[half:], along(-1))


def pack_left(blocks, occupied, row_sizes, k_sizes, out):
    first_k = lax.axis_index("col") * 2
    line = lax.broadcasted_iota(jnp.int32, (BS, BS), 0)
    lane = lax.broadcasted_iota(jnp.int32, (BS, BS), 1)
    slot = jnp.int32(0)
    for i in range(4):
        for k in range(2):
            here = (occupied[k, i] > 0) & (slot < CAP)
            place = slot

            @pl.when(here)
            def _():
                keep = (line < row_sizes[i]) & (lane < k_sizes[first_k + k])
                start = pl.multiple_of(place * BS, BS)
                out[pl.ds(start, BS), :] = jnp.where(keep, blocks[i, k], 0.0)

            where = jnp.where(here, place, -1).astype(jnp.float32)
            out[SLOT_ROWS + 2 * i + k, :] = jnp.full((BS,), where, jnp.float32)
            slot = slot + here.astype(jnp.int32)


def mask_right(blocks, occupied, k_sizes, col_sizes, out):
    used = k_sizes[lax.axis_index("row")]
    line = lax.broadcasted_iota(jnp.int32, (BS, BS), 0)
    lane = lax.broadcasted_iota(jnp.int32, (BS, BS), 1)
    for j in range(4):
        columns = jnp.where(occupied[0, j] > 0, col_sizes[j], 0)
        out[j * BS:(j + 1) * BS, :] = jnp.where((line < used) & (lane < columns), blocks[0, j], 0.0)


def split(value):
    high = value.astype(jnp.bfloat16)
    return high, (value - high.astype(jnp.float32)).astype(jnp.bfloat16)


NEAR = (0, -1, 1, 2)


def prepare_right(along_first, *refs):
    pieces, outs = refs[:5], refs[5:]
    wide = outs[0].shape[1] // BS
    row, core = lax.axis_index("row"), lax.axis_index("col") % 2
    x, y = (row // 4) % 4, row % 4
    for step in range(4):
        for t in range(4):
            ref, at = (pieces[step], t) if step < 3 else (pieces[3 + t // 2], t % 2)
            across, along = (NEAR[t], NEAR[step]) if along_first == "x" else (NEAR[step], NEAR[t])
            from_x, from_y = (x + across + 4) % 4, (y + along + 4) % 4
            foreign = from_y // 2 != core
            start = pl.multiple_of(from_x * 2 * BS + from_y % 2 * BS, BS)
            for other in range(2):

                @pl.when(foreign if other else jnp.logical_not(foreign))
                def _():
                    for j in range(wide):
                        high, low = split(ref[(wide * at + j) * BS:(wide * at + j + 1) * BS, :])
                        outs[2 * other][pl.ds(start, BS), j * BS:(j + 1) * BS] = high
                        outs[2 * other + 1][pl.ds(start, BS), j * BS:(j + 1) * BS] = low


def multiply(last, *refs):
    if last:
        c_filter, before, panel, *rights = refs[:7]
        out, places, copied, left_high, left_low, ready, left = refs[7:]
    else:
        panel, *rights = refs[:5]
        out, places, copied, left_high, left_low = refs[5:]
    zh = lax.axis_index("row") // 16
    placing = [
        pltpu.make_async_copy(panel.at[pl.ds(zl * PAY_ROWS + SLOT_ROWS, 8)], places.at[zl], copied.at[zl])
        for zl in range(NZL)
    ]
    for copy in placing:
        copy.start()
    for copy in placing:
        copy.wait()
    for n in range(8):
        zl = (zh if n < 4 else 1 - zh) * 4 + n % 4
        for i in range(4):
            for k in range(2):
                slot = places[zl, 2 * i + k, 0].astype(jnp.int32)
                start = pl.multiple_of(zl * PAY_ROWS + jnp.maximum(slot, 0) * BS, 8)
                high, low = split(jnp.where(slot >= 0, panel[pl.ds(start, BS), :], 0.0))
                left_high[i * BS:(i + 1) * BS, (2 * n + k) * BS:(2 * n + k + 1) * BS] = high
                left_low[i * BS:(i + 1) * BS, (2 * n + k) * BS:(2 * n + k + 1) * BS] = low
    dot = functools.partial(jnp.dot, preferred_element_type=jnp.float32)
    total = before[...] if last else None
    for family in range(2):
        wide = slice(HALF_ROWS * family, HALF_ROWS * (family + 1))
        right_high, right_low = rights[2 * family][...], rights[2 * family + 1][...]
        part = dot(left_high[:, wide], right_high) + dot(left_high[:, wide], right_low)
        part = part + dot(left_low[:, wide], right_high)
        total = part if total is None else total + part
    if not last:
        out[...] = total
        return
    leaving = []
    for i in range(4):
        for j in range(4):
            value = total[i * BS:(i + 1) * BS, j * BS:(j + 1) * BS]
            ready[i, j] = jnp.where(c_filter[i, j] > 0, value, 0.0)
            leaving.append(pltpu.make_async_copy(ready.at[i, j], out.at[i, j], left.at[i, j]))
            leaving[-1].start()
    for copy in leaving:
        copy.wait()


def add_products(panel, rights, before=None, c_filter=None, flops=1 << 30):
    last = c_filter is not None
    return pl.pallas_call(
        functools.partial(multiply, last),
        out_shape=jax.ShapeDtypeStruct((4, 4, BS, BS) if last else (4 * BS, 4 * BS), jnp.float32),
        in_specs=([SMEM, VMEM] if last else []) + [VMEM] * 5,
        out_specs=ANY if last else VMEM,
        scratch_shapes=[
            pltpu.SMEM((NZL, 8, BS), jnp.float32),
            pltpu.SemaphoreType.DMA((NZL,)),
            pltpu.VMEM((4 * BS, 16 * BS), jnp.bfloat16),
            pltpu.VMEM((4 * BS, 16 * BS), jnp.bfloat16),
        ]
        + ([pltpu.VMEM((4, 4, BS, BS), jnp.float32), pltpu.SemaphoreType.DMA((4, 4))] if last else []),
        compiler_params=pltpu.CompilerParams(vmem_limit_bytes=24 << 20),
        cost_estimate=pl.CostEstimate(flops=flops, bytes_accessed=4 << 20, transcendentals=0),
    )(*((c_filter, before) if last else ()), panel, *rights)


VMEM = pl.BlockSpec(memory_space=pltpu.VMEM)
SMEM = pl.BlockSpec(memory_space=pltpu.SMEM)
ANY = pl.BlockSpec(memory_space=pl.ANY)


def prepare(pieces, along_first):
    return pl.pallas_call(
        functools.partial(prepare_right, along_first),
        out_shape=[jax.ShapeDtypeStruct((HALF_ROWS, 4 * BS), jnp.bfloat16)] * 4,
        in_specs=[VMEM] * 5,
        out_specs=[VMEM] * 4,
        compiler_params=pltpu.CompilerParams(vmem_limit_bytes=24 << 20),
    )(*pieces)


def on_device(a_blocks, b_blocks, a_occupied, b_occupied, c_filter, row_sizes, k_sizes, col_sizes):
    right = pl.pallas_call(
        mask_right,
        out_shape=jax.ShapeDtypeStruct((4 * BS, BS), jnp.float32),
        in_specs=[VMEM, SMEM, SMEM, SMEM],
        out_specs=VMEM,
    )(b_blocks, b_occupied, k_sizes, col_sizes)
    first = [right, *near(right, along_x)]
    partner = send(right, other_half())
    left = pl.pallas_call(
        pack_left,
        out_shape=jax.ShapeDtypeStruct((PAY_ROWS, BS), jnp.float32),
        in_specs=[VMEM, SMEM, SMEM, SMEM],
        out_specs=VMEM,
    )(a_blocks, a_occupied.T, row_sizes, k_sizes)
    same_core = [[zl * NC + core for zl in range(NZL)] for core in range(NC)]
    own = lax.all_gather(left, "col", axis_index_groups=same_core, tiled=True)
    *first, partner = lax.optimization_barrier((*first, partner))
    second = [partner, *near(partner, along_y)]
    first = jnp.concatenate(first)
    second = jnp.concatenate(lax.optimization_barrier(tuple(second)))
    first = [first, *gather_far(first, along_y)]
    second = [second, *gather_far(second, along_x)]
    own, second[1], second[2] = lax.optimization_barrier((own, second[1], second[2]))
    other = send(own, other_core())
    near_by, far_off = prepare(first, "x"), prepare(second, "y")
    part = add_products(own, (*near_by[:2], *far_off[:2]), flops=30 << 30)
    return add_products(other, (*near_by[2:], *far_off[2:]), before=part, c_filter=c_filter)


def solution(mesh):
    placed = (
        P("row", "col", None, None),
        P("row", "col", None, None),
        P("row", "col"),
        P("row", "col"),
        P("row", "col"),
        P("row"),
        P(),
        P("col"),
    )
    return jax.shard_map(
        on_device,
        mesh=mesh,
        in_specs=placed,
        out_specs=P("row", "col", None, None),
        check_vma=False,
    )
```

```python
import functools

import jax
import jax.numpy as jnp
from jax import lax
from jax.experimental import pallas as pl
from jax.experimental.pallas import tpu as pltpu
from jax.sharding import PartitionSpec as P

BS = 128
CAP = 6
SLOT_ROWS = CAP * BS
PAY_ROWS = SLOT_ROWS + 8
HALF_ROWS = 8 * BS
AXES = ("row", "col")
NX, NY, NZH, NZL, NC = 4, 4, 2, 8, 2


def device_pairs(move):
    pairs = []
    for zh in range(NZH):
        for x in range(NX):
            for y in range(NY):
                for zl in range(NZL):
                    for core in range(NC):
                        to = move(zh, x, y, zl, core)
                        pairs.append((linear(zh, x, y, zl, core), linear(*to)))
    return pairs


def linear(zh, x, y, zl, core):
    return (((zh * NX + x) * NY + y) * NZL + zl) * NC + core


def along_x(n):
    return device_pairs(lambda zh, x, y, zl, core: (zh, (x + n) % NX, y, zl, core))


def along_y(n):
    return device_pairs(lambda zh, x, y, zl, core: (zh, x, (y + n) % NY, zl, core))


def other_half():
    return device_pairs(lambda zh, x, y, zl, core: (1 - zh, x, y, zl, core))


def other_core():
    return device_pairs(lambda zh, x, y, zl, core: (zh, x, y, zl, 1 - core))


def send(value, pairs):
    return lax.ppermute(value, AXES, pairs)


def near(block, along):
    return send(block, along(1)), send(block, along(-1)), send(block, along(2))


def gather_far(group, along):
    half = group.shape[0] // 2
    below = send(group, along(1))
    above = send(group, along(-1))
    return below, above, send(below[:half], along(1)), send(above[half:], along(-1))


def pack_left(blocks, occupied, row_sizes, k_sizes, out):
    first_k = lax.axis_index("col") * 2
    line = lax.broadcasted_iota(jnp.int32, (BS, BS), 0)
    lane = lax.broadcasted_iota(jnp.int32, (BS, BS), 1)
    slot = jnp.int32(0)
    for i in range(4):
        for k in range(2):
            here = (occupied[k, i] > 0) & (slot < CAP)
            place = slot

            @pl.when(here)
            def _():
                keep = (line < row_sizes[i]) & (lane < k_sizes[first_k + k])
                start = pl.multiple_of(place * BS, BS)
                out[pl.ds(start, BS), :] = jnp.where(keep, blocks[i, k], 0.0)

            where = jnp.where(here, place, -1).astype(jnp.float32)
            out[SLOT_ROWS + 2 * i + k, :] = jnp.full((BS,), where, jnp.float32)
            slot = slot + here.astype(jnp.int32)


def mask_right(blocks, occupied, k_sizes, col_sizes, out):
    used = k_sizes[lax.axis_index("row")]
    line = lax.broadcasted_iota(jnp.int32, (BS, BS), 0)
    lane = lax.broadcasted_iota(jnp.int32, (BS, BS), 1)
    for j in range(4):
        columns = jnp.where(occupied[0, j] > 0, col_sizes[j], 0)
        out[j * BS:(j + 1) * BS, :] = jnp.where((line < used) & (lane < columns), blocks[0, j], 0.0)


def pack_both(a_blocks, b_blocks, a_occupied, b_occupied, row_sizes, k_sizes, col_sizes, left, right):
    pack_left(a_blocks, a_occupied, row_sizes, k_sizes, left)
    mask_right(b_blocks, b_occupied, k_sizes, col_sizes, right)


def split(value):
    high = value.astype(jnp.bfloat16)
    return high, (value - high.astype(jnp.float32)).astype(jnp.bfloat16)


NEAR = (0, -1, 1, 2)


def prepare_right(along_first, *refs):
    pieces, outs = refs[:5], refs[5:]
    wide = outs[0].shape[1] // BS
    row, core = lax.axis_index("row"), lax.axis_index("col") % 2
    x, y = (row // 4) % 4, row % 4
    for step in range(4):
        for t in range(4):
            ref, at = (pieces[step], t) if step < 3 else (pieces[3 + t // 2], t % 2)
            across, along = (NEAR[t], NEAR[step]) if along_first == "x" else (NEAR[step], NEAR[t])
            from_x, from_y = (x + across + 4) % 4, (y + along + 4) % 4
            foreign = from_y // 2 != core
            start = pl.multiple_of(from_x * 2 * BS + from_y % 2 * BS, BS)
            for other in range(2):

                @pl.when(foreign if other else jnp.logical_not(foreign))
                def _():
                    for j in range(wide):
                        high, low = split(ref[(wide * at + j) * BS:(wide * at + j + 1) * BS, :])
                        outs[2 * other][pl.ds(start, BS), j * BS:(j + 1) * BS] = high
                        outs[2 * other + 1][pl.ds(start, BS), j * BS:(j + 1) * BS] = low


def multiply(last, *refs):
    if last:
        c_filter, before, panel, *rights = refs[:7]
        out, places, copied, left_high, left_low, ready, left = refs[7:]
    else:
        panel, *rights = refs[:5]
        out, places, copied, left_high, left_low = refs[5:]
    zh = lax.axis_index("row") // 16
    placing = [
        pltpu.make_async_copy(panel.at[pl.ds(zl * PAY_ROWS + SLOT_ROWS, 8)], places.at[zl], copied.at[zl])
        for zl in range(NZL)
    ]
    for copy in placing:
        copy.start()
    for copy in placing:
        copy.wait()
    for n in range(8):
        zl = (zh if n < 4 else 1 - zh) * 4 + n % 4
        for i in range(4):
            for k in range(2):
                slot = places[zl, 2 * i + k, 0].astype(jnp.int32)
                start = pl.multiple_of(zl * PAY_ROWS + jnp.maximum(slot, 0) * BS, 8)
                high, low = split(jnp.where(slot >= 0, panel[pl.ds(start, BS), :], 0.0))
                left_high[i * BS:(i + 1) * BS, (2 * n + k) * BS:(2 * n + k + 1) * BS] = high
                left_low[i * BS:(i + 1) * BS, (2 * n + k) * BS:(2 * n + k + 1) * BS] = low
    dot = functools.partial(jnp.dot, preferred_element_type=jnp.float32)
    total = before[...] if last else None
    for family in range(2):
        wide = slice(HALF_ROWS * family, HALF_ROWS * (family + 1))
        right_high, right_low = rights[2 * family][...], rights[2 * family + 1][...]
        part = dot(left_high[:, wide], right_high) + dot(left_high[:, wide], right_low)
        part = part + dot(left_low[:, wide], right_high)
        total = part if total is None else total + part
    if not last:
        out[...] = total
        return
    leaving = []
    for i in range(4):
        for j in range(4):
            value = total[i * BS:(i + 1) * BS, j * BS:(j + 1) * BS]
            ready[i, j] = jnp.where(c_filter[i, j] > 0, value, 0.0)
            leaving.append(pltpu.make_async_copy(ready.at[i, j], out.at[i, j], left.at[i, j]))
            leaving[-1].start()
    for copy in leaving:
        copy.wait()


def add_products(panel, rights, before=None, c_filter=None, flops=1 << 30):
    last = c_filter is not None
    return pl.pallas_call(
        functools.partial(multiply, last),
        out_shape=jax.ShapeDtypeStruct((4, 4, BS, BS) if last else (4 * BS, 4 * BS), jnp.float32),
        in_specs=([SMEM, VMEM] if last else []) + [VMEM] * 5,
        out_specs=ANY if last else VMEM,
        scratch_shapes=[
            pltpu.SMEM((NZL, 8, BS), jnp.float32),
            pltpu.SemaphoreType.DMA((NZL,)),
            pltpu.VMEM((4 * BS, 16 * BS), jnp.bfloat16),
            pltpu.VMEM((4 * BS, 16 * BS), jnp.bfloat16),
        ]
        + ([pltpu.VMEM((4, 4, BS, BS), jnp.float32), pltpu.SemaphoreType.DMA((4, 4))] if last else []),
        compiler_params=pltpu.CompilerParams(vmem_limit_bytes=24 << 20),
        cost_estimate=pl.CostEstimate(flops=flops, bytes_accessed=4 << 20, transcendentals=0),
    )(*((c_filter, before) if last else ()), panel, *rights)


VMEM = pl.BlockSpec(memory_space=pltpu.VMEM)
SMEM = pl.BlockSpec(memory_space=pltpu.SMEM)
ANY = pl.BlockSpec(memory_space=pl.ANY)


def prepare(pieces, along_first):
    return pl.pallas_call(
        functools.partial(prepare_right, along_first),
        out_shape=[jax.ShapeDtypeStruct((HALF_ROWS, 4 * BS), jnp.bfloat16)] * 4,
        in_specs=[VMEM] * 5,
        out_specs=[VMEM] * 4,
        compiler_params=pltpu.CompilerParams(vmem_limit_bytes=24 << 20),
    )(*pieces)


def on_device(a_blocks, b_blocks, a_occupied, b_occupied, c_filter, row_sizes, k_sizes, col_sizes):
    left, right = pl.pallas_call(
        pack_both,
        out_shape=[
            jax.ShapeDtypeStruct((PAY_ROWS, BS), jnp.float32),
            jax.ShapeDtypeStruct((4 * BS, BS), jnp.float32),
        ],
        in_specs=[VMEM, VMEM] + [SMEM] * 5,
        out_specs=[VMEM, VMEM],
    )(a_blocks, b_blocks, a_occupied.T, b_occupied, row_sizes, k_sizes, col_sizes)
    first = [right, *near(right, along_x)]
    partner = send(right, other_half())
    same_core = [[zl * NC + core for zl in range(NZL)] for core in range(NC)]
    own = lax.all_gather(left, "col", axis_index_groups=same_core, tiled=True)
    *first, partner = lax.optimization_barrier((*first, partner))
    second = [partner, *near(partner, along_y)]
    first = jnp.concatenate(first)
    second = jnp.concatenate(lax.optimization_barrier(tuple(second)))
    first = [first, *gather_far(first, along_y)]
    second = [second, *gather_far(second, along_x)]
    own, second[1], second[2] = lax.optimization_barrier((own, second[1], second[2]))
    other = send(own, other_core())
    near_by, far_off = prepare(first, "x"), prepare(second, "y")
    part = add_products(own, (*near_by[:2], *far_off[:2]), flops=30 << 30)
    return add_products(other, (*near_by[2:], *far_off[2:]), before=part, c_filter=c_filter)


def solution(mesh):
    placed = (
        P("row", "col", None, None),
        P("row", "col", None, None),
        P("row", "col"),
        P("row", "col"),
        P("row", "col"),
        P("row"),
        P(),
        P("col"),
    )
    return jax.shard_map(
        on_device,
        mesh=mesh,
        in_specs=placed,
        out_specs=P("row", "col", None, None),
        check_vma=False,
    )
```
